32 devices in a mesh: rows: 8 (over z, y), cols: 4 (over x, core).
Axes of the slice: x: 2, y: 2, z: 4, core: 2. Of those that a mesh axis runs over, the one named last changes fastest.
Arguments:
- prior: bfloat16 [128, 16, 128, 128], P('rows', 'cols'), may hold values from -6 to 6
- candidates: int32 [128, 16], P('rows', 'cols'), may hold values from 0 to 127, as said below
- cross_link: int32 [128], P(('rows', 'cols')), may hold values from 0 to 127, as said below
- a1_blocks: bfloat16 [128, 2, 128, 128], P(('rows', 'cols')), may hold values from -0.375 to 0.375
- a2_blocks: bfloat16 [128, 128, 128], P(('rows', 'cols')), may hold values from -0.5 to 0.5
Outputs:
- similarity: bfloat16 [128, 16, 128, 128], P('rows', 'cols')
The draws below stay inside these ranges and needn't reach their ends.
Inputs may be any that keep to these rules, and one draw needn't show every extreme that they name: Target block t lies in target slab t // 16 and quarter (t // 4) % 4; a candidate in columns q * 4 to (q + 1) * 4 - 1 names a target of quarter q. The candidates of one row block in one quarter lie in distinct target slabs. Of the candidates held by one device, at most 8 lie in one target slab, and some slab gets exactly 8; every target slab gets 16 * 4 candidates of its quarter from all source slabs together. `cross_link`: the linked row block of a row block in slab r lies in the last half of the row blocks of slab (r + 1) % 8.
All inputs are finite; a program needn't handle non-finite values.
Results may differ from the reference program's by a relative error of at most 0.006.
Values may be sent and summed in bfloat16 or wider, within the bound.
No kernel may reach another device: no remote copies, remote signals or barrier semaphores. Data moves between devices by JAX's collectives and lax.ppermute only.
A program may use at most 64 MiB of HBM per device.

```python
import jax
import jax.numpy as jnp
from jax import lax

B = 128
K = 16
RBD = 16
KQ = 4
TBD = 4
RB = 128
N_ROWS = 8
N_COLS = 4


def draw_candidates(key, part):
    key_shift = jax.random.fold_in(key, 11)
    key_table = jax.random.fold_in(key, 12)
    key_order = jax.random.fold_in(key, 13)
    row_index = jnp.arange(RB, dtype=jnp.int32)
    column_step = jnp.arange(KQ, dtype=jnp.int32)
    quarter = jnp.arange(N_COLS, dtype=jnp.int32)[None, :, None]
    shifts = jax.random.randint(key_shift, (N_COLS,), 0, N_ROWS, dtype=jnp.int32)
    table = jax.random.randint(key_table, (N_COLS, N_ROWS * TBD), 0, TBD, dtype=jnp.int32)
    code = row_index[:, None, None] + (RBD + 1) * column_step[None, None, :]
    code = jnp.broadcast_to(code, (RB, N_COLS, KQ))
    dest_slab = (code + shifts[None, :, None]) % N_ROWS
    local_index = table[jnp.broadcast_to(quarter, (RB, N_COLS, KQ)), code % (N_ROWS * TBD)]
    target = dest_slab * (N_COLS * TBD) + quarter * TBD + local_index
    scores = jax.random.randint(key_order, (RB, N_COLS, KQ), 0, 1048576, dtype=jnp.int32) * KQ + column_step[None, None, :]
    order = jnp.argsort(scores, axis=2)
    target = jnp.take_along_axis(target, order, axis=2)
    return target.reshape(RB, K).astype(jnp.int32)


def draw_cross_link(key, part):
    key_coin = jax.random.fold_in(key, 21)
    key_pick = jax.random.fold_in(key, 22)
    row_index = jnp.arange(RB, dtype=jnp.int32)
    slab_index = row_index // RBD
    within_slab = row_index % RBD
    next_slab = (slab_index + 1) % N_ROWS
    coin = jax.random.randint(key_coin, (RB,), 0, 4, dtype=jnp.int32)
    random_pick = jax.random.randint(key_pick, (RB,), RBD // 2, RBD, dtype=jnp.int32)
    aligned = (within_slab >= RBD // 2 - 1) & (within_slab <= RBD - 2) & (coin > 0)
    chosen_row = jnp.where(aligned, within_slab + 1, random_pick)
    return (next_slab * RBD + chosen_row).astype(jnp.int32)


def levels(rng, shape, shards, least, largest):
    def one(position, shards_of):
        steps = jax.random.uniform(jax.random.fold_in(jax.random.fold_in(rng, 6), position), (shards_of,), jnp.float32, least / len(shards), largest / len(shards))
        return jnp.repeat(jnp.exp(steps), shape[position] // shards_of).reshape((-1,) + (1,) * (len(shape) - position - 1))

    gain = one(*shards[0])
    for cut in shards[1:]:
        gain = gain * one(*cut)
    return gain


def centred(rng, dims, deviation, limit, split=(), held_as=jnp.bfloat16):
    result = deviation * jax.random.normal(rng, dims, jnp.float32)
    if split:
        result = result * levels(rng, dims, split, -0.22, 0.18)
    return jnp.clip(result, -limit, limit).astype(held_as)


def setup_inputs(seed: int = 0) -> dict:
    seeds = jax.random.split(jax.random.key(seed), 6)
    prior = centred(seeds[0], (RB, K, B, B), 1.0, 6.0, ((0, 8), (1, 4)))
    candidates = draw_candidates(jax.random.fold_in(seeds[5], 71), 0)
    cross_link = draw_cross_link(jax.random.fold_in(seeds[5], 71), 0)
    a1_blocks = centred(seeds[3], (RB, 2, B, B), (2 * B) ** -0.5, 0.375, ((0, 32),))
    a2_blocks = centred(seeds[4], (RB, B, B), B ** -0.5, 0.5, ((0, 32),))
    return {"prior": prior, "candidates": candidates, "cross_link": cross_link, "a1_blocks": a1_blocks, "a2_blocks": a2_blocks}


mixing = 0.75


def left_slab(values, offset, prior_ids, cross_link, a1_blocks):
    slab_vals = lax.dynamic_slice_in_dim(values, offset, RBD, 0)
    slab_ids = lax.dynamic_slice_in_dim(prior_ids, offset, RBD, 0)
    adjacency = lax.dynamic_slice_in_dim(a1_blocks, offset, RBD, 0)
    neighbour = lax.dynamic_slice_in_dim(cross_link, offset, RBD, 0)
    nb_values = values[neighbour]
    nb_ids = prior_ids[neighbour]
    matches = slab_ids[:, :, None] == nb_ids[:, None, :]
    chosen = jnp.sum(jnp.where(matches, jnp.arange(K, dtype=jnp.int32)[None, None, :], 0), axis=2).astype(jnp.int32)
    found = jnp.any(matches, axis=2)
    picked = jnp.take_along_axis(nb_values, chosen[:, :, None, None], axis=1)
    picked = jnp.where(found[:, :, None, None], picked, jnp.zeros_like(picked))
    own_term = jnp.einsum("ixy,ikyz->ikxz", adjacency[:, 0].astype(jnp.float32), slab_vals.astype(jnp.float32), precision=lax.Precision.HIGHEST)
    cross_term = jnp.einsum("ixy,ikyz->ikxz", adjacency[:, 1].astype(jnp.float32), picked.astype(jnp.float32), precision=lax.Precision.HIGHEST)
    return own_term + cross_term


def right_blocks(slab_vals, slab_ids, a2_blocks):
    target_blocks = a2_blocks[slab_ids]
    return jnp.einsum("ikxy,ikzy->ikxz", slab_vals.astype(jnp.float32), target_blocks.astype(jnp.float32), precision=lax.Precision.HIGHEST)


def reference(prior, candidates, cross_link, a1_blocks, a2_blocks):
    offsets = jnp.arange(N_ROWS, dtype=jnp.int32) * RBD

    def phase_one(offset):
        return left_slab(prior, offset, candidates, cross_link, a1_blocks).astype(jnp.bfloat16)

    first = lax.map(phase_one, offsets).reshape(RB, K, B, B)

    def phase_two(offset):
        slab_first = lax.dynamic_slice_in_dim(first, offset, RBD, 0)
        slab_prior = lax.dynamic_slice_in_dim(prior, offset, RBD, 0)
        slab_ids = lax.dynamic_slice_in_dim(candidates, offset, RBD, 0)
        image = right_blocks(slab_first, slab_ids, a2_blocks)
        swept = (mixing * image + (1.0 - mixing) * slab_prior.astype(jnp.float32)).astype(jnp.bfloat16)
        return right_blocks(swept, slab_ids, a2_blocks).astype(jnp.bfloat16)

    carried = lax.map(phase_two, offsets).reshape(RB, K, B, B)

    def phase_three(offset):
        slab_prior = lax.dynamic_slice_in_dim(prior, offset, RBD, 0)
        image = left_slab(carried, offset, candidates, cross_link, a1_blocks)
        return (mixing * image + (1.0 - mixing) * slab_prior.astype(jnp.float32)).astype(jnp.bfloat16)

    return lax.map(phase_three, offsets).reshape(RB, K, B, B)
```

```python
import functools

import jax
import jax.numpy as jnp
from jax import lax
from jax.experimental import pallas as pl
from jax.experimental.pallas import tpu as pltpu
from jax.sharding import PartitionSpec as P

mixing = 0.75
pad = 16
chunk_count = 2


def bits_of(count):
    return count.bit_length() - 1


def exchange(array, axis, mask):
    count = lax.axis_size(axis)
    return lax.ppermute(array, axis, [(i, i ^ mask) for i in range(count)])


def gathered_place(distance, order):
    place = jnp.zeros_like(distance)
    for step, mask in enumerate(order):
        place = place + jnp.where((distance & mask) != 0, 1 << step, 0)
    return place


def transpose_kernel(src, dst):
    for t in range(src.shape[0]):
        dst[t] = src[t].T


def sweep_kernel(
    chunks, rows, per_quarter, block, half, per_step, own_rows, share_rows, next_rows,
    index, p_own, *refs,
):
    near = refs[:chunks]
    passed = refs[chunks : 2 * chunks]
    far = refs[2 * chunks : 3 * chunks]
    a_ref, t_ref, out_ref, p1, p2, fj, sems = refs[3 * chunks :]
    count = half * per_quarter
    wide = per_quarter * block
    step = pl.program_id(0)
    at_a = 0
    at_b = rows
    at_idx1 = at_b + half
    at_idx2 = at_idx1 + rows * per_quarter
    at_t = at_idx2 + count
    at_even = at_t + rows * per_quarter

    def weights(offset):
        start = pl.multiple_of(offset, pad)
        left = a_ref[pl.ds(start, block), :]
        right = a_ref[pl.ds(pl.multiple_of(start + block, pad), block), :]
        return jnp.concatenate([left, right], axis=1)

    def side(blocks):
        return jnp.concatenate(blocks, axis=1)

    def blk(ref, n):
        return ref[pl.ds(pl.multiple_of(n * block, block), block), :]

    @pl.when(step == 0)
    def _():
        each = count // chunks * block
        zero = jnp.zeros((block, block), jnp.bfloat16)
        for ref in (p1, p2, fj):
            ref[pl.ds(count * block, block), :] = zero

        def copies(sources, c, target, sem):
            return pltpu.make_async_copy(
                sources[c].at[pl.ds(0, each), :], target.at[pl.ds(c * each, each), :], sem
            )

        even = index[at_even] == 1

        @pl.when(even)
        def _():
            for c in range(chunks):
                copies(near, c, p1, sems.at[0, c]).start()

        @pl.when(jnp.logical_not(even))
        def _():
            for c in range(chunks):
                copies(passed, c, p1, sems.at[0, c]).start()

        for c in range(chunks):
            copies(far, c, p2, sems.at[1, c]).start()
        for c in range(chunks):
            copies(near, c, p1, sems.at[0, c]).wait()
            copies(far, c, p2, sems.at[1, c]).wait()
        for j in range(half):
            w = weights(index[at_b + j])
            top = side([blk(p1, j * per_quarter + k) for k in range(per_quarter)])
            low = side([blk(p2, index[at_idx2 + j * per_quarter + k]) for k in range(per_quarter)])
            got = jnp.dot(w, jnp.concatenate([top, low], axis=0), preferred_element_type=jnp.float32)
            got = got.astype(jnp.bfloat16)
            for k in range(per_quarter):
                fj[pl.ds((j * per_quarter + k) * block, block), :] = got[:, k * block : (k + 1) * block]

    for u in range(per_step):
        i = step * per_step + u
        w = weights(index[at_a + i])
        picks = [index[at_idx1 + i * per_quarter + k] for k in range(per_quarter)]
        own = side([p_own[u, k] for k in range(per_quarter)])
        cross = side([blk(p1, n) for n in picks])
        first = jnp.dot(w, jnp.concatenate([own, cross], axis=0), preferred_element_type=jnp.float32)
        cross2 = side([blk(fj, n) for n in picks])
        second = jnp.dot(
            w,
            jnp.concatenate([first.astype(jnp.bfloat16), cross2], axis=0),
            preferred_element_type=jnp.float32,
        ).astype(jnp.bfloat16)
        for k in range(per_quarter):
            cut = slice(k * block, (k + 1) * block)
            t = t_ref[index[at_t + i * per_quarter + k]]
            image = jnp.dot(second[:, cut], t, preferred_element_type=jnp.float32)
            swept = (mixing * image + (1.0 - mixing) * first[:, cut]).astype(jnp.bfloat16)
            last = jnp.dot(swept, t, preferred_element_type=jnp.float32)
            out_ref[u, k] = (
                mixing * last + (1.0 - mixing) * p_own[u, k].astype(jnp.float32)
            ).astype(jnp.bfloat16)


def tile_of(values):
    return jnp.pad(values.astype(jnp.bfloat16)[None, :], ((0, pad - 1), (0, 128 - values.shape[0])))


def local(prior, candidates, cross_link, a1_blocks, a2_blocks):
    rows, per_quarter, block = prior.shape[:3]
    here = a2_blocks.shape[0]
    slabs = lax.axis_size("rows")
    quarters = lax.axis_size("cols")
    slab = lax.axis_index("rows")
    quarter = lax.axis_index("cols")
    half = rows // 2
    share = a1_blocks.shape[0]
    part = share // 2
    chunks = chunk_count
    each = half // chunks
    count = half * per_quarter

    target_slab = candidates // (quarters * here)
    target_local = candidates % here
    codes = target_slab * here + target_local
    id_tile = tile_of(
        jnp.concatenate([target_slab[half:].reshape(-1), target_local[half:].reshape(-1)])
    )
    sent = []
    for c in range(chunks):
        piece = prior[half + c * each : half + (c + 1) * each].reshape(-1, block)
        sent.append(jnp.concatenate([piece, id_tile], axis=0) if c == 0 else piece)
    links = cross_link % rows - half
    own_weights = jnp.concatenate([a1_blocks.reshape(-1, block), tile_of(links)], axis=0)
    parts = [
        jnp.concatenate(
            [a1_blocks[c * part : (c + 1) * part].reshape(-1, block), tile_of(links[c * part : (c + 1) * part])],
            axis=0,
        )
        for c in range(2)
    ]

    by_two = [(i, (i - 2) % slabs) for i in range(slabs)]
    to_even = [(i + 1, i) for i in range(0, slabs, 2)]
    to_odd = [(i, i + 1) for i in range(0, slabs, 2)]
    far = [lax.ppermute(x, "rows", by_two) for x in sent]
    near = [lax.ppermute(x, "rows", to_even) for x in sent]
    passed = [lax.ppermute(x, "rows", to_odd) for x in far]

    both = ("rows", "cols")
    upper = range(quarters // 2, quarters)
    kept = [(((s + 1) % slabs) * quarters + q, s * quarters + q) for s in range(slabs) for q in upper]
    moved = [
        (((s + 1) % slabs) * quarters + q, s * quarters + q - quarters // 2)
        for s in range(slabs)
        for q in upper
    ]
    next_part = jnp.where(
        quarter >= quarters // 2,
        lax.ppermute(parts[0], both, kept),
        lax.ppermute(parts[1], both, moved),
    )
    weights = jnp.concatenate([own_weights, next_part], axis=0)
    own_rows, next_rows = own_weights.shape[0], next_part.shape[0]
    share_rows = own_rows + next_rows
    column_order = [1 << b for b in reversed(range(bits_of(quarters)))]
    for mask in column_order:
        weights = jnp.concatenate([weights, exchange(weights, "cols", mask)], axis=0)

    targets = pl.pallas_call(
        transpose_kernel, out_shape=jax.ShapeDtypeStruct(a2_blocks.shape, a2_blocks.dtype)
    )(a2_blocks)
    row_order = [1 << b for b in range(1, bits_of(slabs))] + [1]
    for mask in row_order:
        targets = jnp.concatenate([targets, exchange(targets, "rows", mask)], axis=0)

    def codes_in(buffer):
        values = buffer[-pad, : 2 * count].astype(jnp.int32)
        return (values[:count] * here + values[count:]).reshape(half, per_quarter)

    even = slab % 2 == 0
    codes_far = codes_in(far[0])
    codes_near = jnp.where(even, codes_in(near[0]), codes_in(passed[0]))
    tiles = weights.reshape(quarters, share_rows, block)
    row_quarter = jnp.arange(quarters, dtype=jnp.int32)
    place = gathered_place(row_quarter ^ quarter, column_order)
    link_own = tiles[:, own_rows - pad, :share].astype(jnp.int32)[place].reshape(-1)
    offset_own = (
        place[:, None] * share_rows + jnp.arange(share, dtype=jnp.int32)[None, :] * 2 * block
    ).reshape(-1)
    next_index = jnp.arange(half, dtype=jnp.int32)
    source = quarters // 2 + next_index // share
    inside = next_index % share
    holder = jnp.where(inside < part, source, source - quarters // 2)
    holder_place = gathered_place(holder ^ quarter, column_order)
    inside = inside % part
    link_next = tiles[:, share_rows - pad, :part].astype(jnp.int32)[holder_place, inside]
    offset_next = holder_place * share_rows + own_rows + inside * 2 * block

    def picked(mine, theirs, link):
        same = mine[:, :, None] == theirs[link][:, None, :]
        column = jnp.sum(
            jnp.where(same, jnp.arange(per_quarter, dtype=jnp.int32)[None, None, :], 0), axis=2
        )
        return jnp.where(jnp.any(same, axis=2), link[:, None] * per_quarter + column, count)

    pick_own = picked(codes, codes_near, link_own)
    pick_next = picked(codes_near, codes_far, link_next)
    target_place = gathered_place(target_slab ^ slab, row_order) * here + target_local
    index = jnp.concatenate(
        [
            offset_own,
            offset_next,
            pick_own.reshape(-1),
            pick_next.reshape(-1),
            target_place.reshape(-1),
            even.astype(jnp.int32)[None],
        ]
    )

    steps = 4
    per_step = rows // steps
    anywhere = pl.BlockSpec(memory_space=pl.ANY)
    whole = pl.BlockSpec(memory_space=pltpu.VMEM)
    row_spec = pl.BlockSpec((per_step, per_quarter, block, block), lambda s, _: (s, 0, 0, 0))
    scratch = pltpu.VMEM(((count + 1) * block, block), jnp.bfloat16)
    kernel = functools.partial(
        sweep_kernel, chunks, rows, per_quarter, block, half, per_step, own_rows, share_rows, next_rows
    )
    return pl.pallas_call(
        kernel,
        grid_spec=pltpu.PrefetchScalarGridSpec(
            num_scalar_prefetch=1,
            grid=(steps,),
            in_specs=[row_spec] + [anywhere] * (3 * chunks) + [whole, whole],
            out_specs=row_spec,
            scratch_shapes=[scratch, scratch, scratch, pltpu.SemaphoreType.DMA((2, chunks))],
        ),
        out_shape=jax.ShapeDtypeStruct(prior.shape, prior.dtype),
        compiler_params=pltpu.CompilerParams(
            vmem_limit_bytes=48 * 1024 * 1024, dimension_semantics=("arbitrary",)
        ),
        cost_estimate=pl.CostEstimate(flops=3 * 10**9, bytes_accessed=8 * 2**20, transcendentals=0),
    )(index, prior, *near, *passed, *far, weights, targets)


def solution(mesh):
    placed = (
        P("rows", "cols", None, None),
        P("rows", "cols"),
        P(("rows", "cols")),
        P(("rows", "cols"), None, None, None),
        P(("rows", "cols"), None, None),
    )
    return jax.shard_map(
        local, mesh=mesh, in_specs=placed, out_specs=P("rows", "cols", None, None), check_vma=False
    )
```

```python
import functools

import jax
import jax.numpy as jnp
from jax import lax
from jax.experimental import pallas as pl
from jax.experimental.pallas import tpu as pltpu
from jax.sharding import PartitionSpec as P

mixing = 0.75
pad = 16
plan = {'sizes': (4, 4),
 'gates': {'Y1': ['Y0'], 'T': ['I1'], 'I1': ['Z0'], 'I2': ['Z0']},
 'order': ['Z0', 'I', 'Z1', 'T', 'KM', 'Y0', 'X', 'Y1', 'E1', 'E2', 'E3'],
 'cost': 0,
 'groups': 4,
 'vmem': 48,
 'any': True}


def bits_of(count):
    return count.bit_length() - 1


def exchange(array, axis, mask):
    count = lax.axis_size(axis)
    return lax.ppermute(array, axis, [(i, i ^ mask) for i in range(count)])


def taken_from(array, axis, ahead):
    count = lax.axis_size(axis)
    return lax.ppermute(array, axis, [(i, (i - ahead) % count) for i in range(count)])


def after(array, *others):
    return lax.optimization_barrier((array, *others))[0] if others else array


def gathered_place(distance, order):
    place = jnp.zeros_like(distance)
    for step, mask in enumerate(order):
        place = place + jnp.where((distance & mask) != 0, 1 << step, 0)
    return place


def transpose_kernel(src, dst):
    for t in range(src.shape[0]):
        dst[t] = src[t].T


def tile_of(values):
    return jnp.pad(values.astype(jnp.bfloat16)[None, :], ((0, pad - 1), (0, 128 - values.shape[0])))


def row_slice(ref, start, size):
    return ref[pl.ds(pl.multiple_of(start, pad), size), :]


def side(blocks):
    return jnp.concatenate(blocks, axis=1)


def assemble(pieces, sems):
    copies = [
        pltpu.make_async_copy(
            source.at[pl.ds(at, size), :], target.at[pl.ds(to, size), :], sems.at[n]
        )
        for n, (source, at, size, target, to) in enumerate(pieces)
    ]
    for copy in copies:
        copy.start()
    return copies


def left_kernel(layout, rows, per_quarter, block, half, index, prior, *refs):
    first, second, p1, p2, weights, first_next, sems = refs[-7:]
    targets = (p1, p2, weights)
    count = half * per_quarter
    copies = assemble(
        [(refs[n], at, size, targets[which], to) for n, at, size, which, to in layout], sems
    )
    at_next = rows
    at_pick = at_next + half
    at_pick_next = at_pick + rows * per_quarter

    def row_weights(offset):
        return side([row_slice(weights, offset, block), row_slice(weights, offset + block, block)])

    def blk(ref, n):
        return ref[pl.ds(pl.multiple_of(n * block, block), block), :]

    zero = jnp.zeros((block, block), jnp.bfloat16)
    for ref in (p1, p2, first_next):
        ref[pl.ds(count * block, block), :] = zero
    for copy in copies:
        copy.wait()
    for j in range(half):
        top = side([blk(p1, j * per_quarter + k) for k in range(per_quarter)])
        low = side([blk(p2, index[at_pick_next + j * per_quarter + k]) for k in range(per_quarter)])
        got = jnp.dot(
            row_weights(index[at_next + j]),
            jnp.concatenate([top, low], axis=0),
            preferred_element_type=jnp.float32,
        ).astype(jnp.bfloat16)
        for k in range(per_quarter):
            first_next[pl.ds((j * per_quarter + k) * block, block), :] = got[:, k * block : (k + 1) * block]
    for i in range(rows):
        own = side([prior[i, k] for k in range(per_quarter)])
        cross = side([blk(p1, index[at_pick + i * per_quarter + k]) for k in range(per_quarter)])
        first[i] = jnp.dot(
            row_weights(index[i]),
            jnp.concatenate([own, cross], axis=0),
            preferred_element_type=jnp.float32,
        ).astype(jnp.bfloat16)
    for i in range(rows):
        cross = side([blk(first_next, index[at_pick + i * per_quarter + k]) for k in range(per_quarter)])
        second[i] = jnp.dot(
            row_weights(index[i]),
            jnp.concatenate([first[i], cross], axis=0),
            preferred_element_type=jnp.float32,
        ).astype(jnp.bfloat16)


def right_kernel(layout, rows, per_quarter, block, groups, index, prior, first, second, *refs):
    out, targets, swept, result, sems, out_sems = refs[-6:]
    copies = assemble([(refs[n], at, size, targets, to) for n, at, size, to in layout], sems)
    for copy in copies:
        copy.wait()

    def target(i, k):
        return targets[pl.ds(pl.multiple_of(index[i * per_quarter + k] * block, block), block), :]

    def cut(k):
        return slice(k * block, (k + 1) * block)

    per_group = rows // groups
    sent = []
    for g in range(groups):
        mine = range(g * per_group, (g + 1) * per_group)
        for i in mine:
            for k in range(per_quarter):
                image = jnp.dot(second[i, :, cut(k)], target(i, k), preferred_element_type=jnp.float32)
                swept[i, :, cut(k)] = (
                    mixing * image + (1.0 - mixing) * first[i, :, cut(k)].astype(jnp.float32)
                ).astype(jnp.bfloat16)
        for i in mine:
            for k in range(per_quarter):
                last = jnp.dot(swept[i, :, cut(k)], target(i, k), preferred_element_type=jnp.float32)
                result[i, k] = (
                    mixing * last + (1.0 - mixing) * prior[i, k].astype(jnp.float32)
                ).astype(jnp.bfloat16)
        span = pl.ds(g * per_group, per_group)
        copy = pltpu.make_async_copy(result.at[span], out.at[span], out_sems.at[g])
        copy.start()
        sent.append(copy)
    for copy in sent:
        copy.wait()


def local(prior, candidates, cross_link, a1_blocks, a2_blocks):
    rows, per_quarter, block = prior.shape[:3]
    here = a2_blocks.shape[0]
    slabs = lax.axis_size("rows")
    quarters = lax.axis_size("cols")
    slab = lax.axis_index("rows")
    quarter = lax.axis_index("cols")
    half = rows // 2
    share = a1_blocks.shape[0]
    part = share // 2
    count = half * per_quarter
    sizes = plan["sizes"]
    chunks = len(sizes)
    starts = [sum(sizes[:c]) for c in range(chunks)]
    even = slab % 2 == 0
    there = {}

    def gated(array, name):
        return after(array, *[there[n] for n in plan["gates"].get(name, ())])

    def record(name, array):
        there[name] = array
        return array

    target_slab = candidates >> bits_of(quarters * here)
    target_local = candidates & (here - 1)
    t_rows = here * block
    anywhere = pl.BlockSpec(memory_space=pl.ANY)
    whole = pl.BlockSpec(memory_space=pltpu.VMEM)
    scalars = pl.BlockSpec(memory_space=pltpu.SMEM)

    mine = [
        prior[half + starts[c] : half + starts[c] + sizes[c]].reshape(-1, block) for c in range(chunks)
    ]
    links = cross_link % rows - half
    own_weights = jnp.concatenate([a1_blocks.reshape(-1, block), tile_of(links)], axis=0)
    parts = [
        jnp.concatenate(
            [a1_blocks[c * part : (c + 1) * part].reshape(-1, block), tile_of(links[c * part : (c + 1) * part])],
            axis=0,
        )
        for c in range(2)
    ]
    turned = pl.pallas_call(
        transpose_kernel, out_shape=jax.ShapeDtypeStruct(a2_blocks.shape, a2_blocks.dtype)
    )(a2_blocks).reshape(-1, block)

    far, near = {}, {}
    column = {}

    def do_far(c):
        payload = mine[c]
        got = taken_from(gated(payload, "Z%d" % c), "rows", 2)
        far[c] = record("Z%d" % c, got)

    def do_near(c):
        payload = jnp.where(even, far[c], mine[c])
        near[c] = record("Y%d" % c, exchange(gated(payload, "Y%d" % c), "rows", 1))

    def do_pair():
        got = record("T", exchange(gated(turned, "T"), "rows", 1))
        column[0] = jnp.concatenate([turned, got], axis=0)

    def do_column(d):
        column[d] = record("E%d" % d, taken_from(gated(column[0], "E%d" % d), "rows", 2 * d))

    both = ("rows", "cols")
    upper = range(quarters // 2, quarters)
    kept = [(((s + 1) % slabs) * quarters + q, s * quarters + q) for s in range(slabs) for q in upper]
    moved = [
        (((s + 1) % slabs) * quarters + q, s * quarters + q - quarters // 2)
        for s in range(slabs)
        for q in upper
    ]
    column_order = [1 << b for b in reversed(range(bits_of(quarters)))]
    w = {}

    def do_next():
        w["kept"] = record("K", lax.ppermute(gated(parts[0], "K"), both, kept))
        w["moved"] = record("M", lax.ppermute(gated(parts[1], "M"), both, moved))

    def do_columns():
        next_part = jnp.where(quarter >= quarters // 2, w["kept"], w["moved"])
        base = jnp.concatenate([own_weights, next_part], axis=0)
        w["pieces"] = [base]
        for n, mask in enumerate(column_order):
            got = record("X%d" % n, exchange(gated(base, "X%d" % n), "cols", mask))
            w["pieces"].append(got)
            base = jnp.concatenate([base, got], axis=0)
        w["all"] = base

    few = slabs == 8
    if few:
        distances = range(1, slabs // 2)
    else:
        distances = ()

    def do_ids():
        for ahead in (1, 2):
            record("I%d" % ahead, taken_from(gated(candidates[half:], "I%d" % ahead), "rows", ahead))

    for name in plan["order"]:
        if name[0] == "Z":
            do_far(int(name[1:]))
        elif name[0] == "Y":
            do_near(int(name[1:]))
        elif name == "I":
            do_ids()
        elif name == "KM":
            do_next()
        elif name == "X":
            do_columns()
        elif name[0] == "E" and few:
            do_column(int(name[1:]))
        elif name == "T" and few:
            do_pair()
    row_order = [1 << b for b in range(1, bits_of(slabs))]
    if not few:
        base = turned
        for mask in row_order:
            base = jnp.concatenate([base, exchange(base, "rows", mask)], axis=0)
        swapped = exchange(base, "rows", 1)

    own_rows = own_weights.shape[0]
    share_rows = own_rows + parts[0].shape[0]
    tiles = w["all"].reshape(quarters, share_rows, block)
    row_quarter = jnp.arange(quarters, dtype=jnp.int32)
    place = gathered_place(row_quarter ^ quarter, column_order)

    def taken(table, at):
        same = at[..., None] == jnp.arange(table.shape[0], dtype=jnp.int32)
        return jnp.sum(
            jnp.where(same.reshape(same.shape + (1,) * (table.ndim - 1)), table, 0), axis=at.ndim
        )

    link_own = taken(tiles[:, own_rows - pad, :share].astype(jnp.int32), place).reshape(-1)
    offset_own = (
        place[:, None] * share_rows + jnp.arange(share, dtype=jnp.int32)[None, :] * 2 * block
    ).reshape(-1)
    next_index = jnp.arange(half, dtype=jnp.int32)
    source = quarters // 2 + next_index // share
    inside = next_index % share
    holder = jnp.where(inside < part, source, source - quarters // 2)
    holder_place = gathered_place(holder ^ quarter, column_order)
    inside = inside % part
    link_next = taken(
        tiles[:, share_rows - pad, :part].astype(jnp.int32).reshape(-1), holder_place * part + inside
    )
    offset_next = holder_place * share_rows + own_rows + inside * 2 * block

    def picked(ours, theirs, link):
        same = ours[:, :, None] == taken(theirs, link)[:, None, :]
        which = jnp.sum(
            jnp.where(same, jnp.arange(per_quarter, dtype=jnp.int32)[None, None, :], 0), axis=2
        )
        return jnp.where(jnp.any(same, axis=2), link[:, None] * per_quarter + which, count)

    pick_own = picked(candidates, there["I1"], link_own)
    pick_next = picked(there["I1"], there["I2"], link_next)
    index = jnp.concatenate(
        [offset_own, offset_next, pick_own.reshape(-1), pick_next.reshape(-1)]
    )
    odd_one = (target_slab ^ slab) & 1
    base_slab = slab ^ odd_one
    if few:
        ahead = ((target_slab - base_slab) % slabs) // 2
    else:
        ahead = gathered_place(target_slab ^ base_slab, row_order)
    target_place = (odd_one * (slabs // 2) + ahead) * here + target_local
    t_index = target_place.reshape(-1)

    params = pltpu.CompilerParams(vmem_limit_bytes=plan["vmem"] * 1024 * 1024)

    plan_space = anywhere if plan["any"] else whole
    arrays, layout = [], []

    def piece(array, at, size, *where):
        for n, known in enumerate(arrays):
            if known is array:
                break
        else:
            n = len(arrays)
            arrays.append(array)
        layout.append((n, at, size, *where))

    for c in range(chunks):
        size = sizes[c] * per_quarter * block
        piece(near[c], 0, size, 0, starts[c] * per_quarter * block)
        piece(far[c], 0, size, 1, starts[c] * per_quarter * block)
    to = 0
    for array in w["pieces"]:
        piece(array, 0, array.shape[0], 2, to)
        to += array.shape[0]
    wide = jax.ShapeDtypeStruct((rows, block, per_quarter * block), jnp.bfloat16)
    stack = pltpu.VMEM(((count + 1) * block, block), jnp.bfloat16)
    first, second = pl.pallas_call(
        functools.partial(left_kernel, tuple(layout), rows, per_quarter, block, half),
        in_specs=[scalars, whole] + [plan_space] * len(arrays),
        out_specs=[whole, whole],
        out_shape=[wide, wide],
        scratch_shapes=[
            stack,
            stack,
            pltpu.VMEM((to, block), jnp.bfloat16),
            stack,
            pltpu.SemaphoreType.DMA((len(layout),)),
        ],
        compiler_params=params,
        cost_estimate=pl.CostEstimate(flops=plan["cost"] * 10**9, bytes_accessed=8 * 2**20, transcendentals=0),
    )(index, prior, *arrays)

    arrays, layout = [], []
    if few:
        for d in range(slabs // 2):
            piece(column[d], 0, t_rows, d * t_rows)
            piece(column[d], t_rows, t_rows, (slabs // 2 + d) * t_rows)
    else:
        piece(base, 0, base.shape[0], 0)
        piece(swapped, 0, base.shape[0], base.shape[0])
    groups = plan["groups"]
    return pl.pallas_call(
        functools.partial(right_kernel, tuple(layout), rows, per_quarter, block, groups),
        in_specs=[scalars, whole, whole, whole] + [plan_space] * len(arrays),
        out_specs=anywhere,
        out_shape=jax.ShapeDtypeStruct(prior.shape, prior.dtype),
        scratch_shapes=[
            pltpu.VMEM((slabs * t_rows, block), jnp.bfloat16),
            pltpu.VMEM(wide.shape, jnp.bfloat16),
            pltpu.VMEM(prior.shape, jnp.bfloat16),
            pltpu.SemaphoreType.DMA((len(layout),)),
            pltpu.SemaphoreType.DMA((groups,)),
        ],
        compiler_params=params,
        cost_estimate=pl.CostEstimate(flops=10**9, bytes_accessed=8 * 2**20, transcendentals=0),
    )(t_index, prior, first, second, *arrays)


def solution(mesh):
    placed = (
        P("rows", "cols", None, None),
        P("rows", "cols"),
        P(("rows", "cols")),
        P(("rows", "cols"), None, None, None),
        P(("rows", "cols"), None, None),
    )
    return jax.shard_map(
        local, mesh=mesh, in_specs=placed, out_specs=P("rows", "cols", None, None), check_vma=False
    )
```

```python
import functools

import jax
import jax.numpy as jnp
from jax import lax
from jax.experimental import pallas as pl
from jax.experimental.pallas import tpu as pltpu
from jax.sharding import PartitionSpec as P

mixing = 0.75
pad = 16
plan = {'sizes': (4, 4),
 'gates': {'Y1': ['Y0'], 'T': ['Z0'], 'I1': ['T'], 'I2': ['T'], 'E1': ['Y0'], 'E3': ['Y0']},
 'order': ['Z0', 'Z1', 'KM', 'T', 'I', 'X', 'Y0', 'Y1', 'E1', 'E2', 'E3'],
 'cost': 0,
 'groups': 4,
 'vmem': 48,
 'any': True,
 'parts_later': False}


def bits_of(count):
    return count.bit_length() - 1


def exchange(array, axis, mask):
    count = lax.axis_size(axis)
    return lax.ppermute(array, axis, [(i, i ^ mask) for i in range(count)])


def taken_from(array, axis, ahead):
    count = lax.axis_size(axis)
    return lax.ppermute(array, axis, [(i, (i - ahead) % count) for i in range(count)])


def after(array, *others):
    return lax.optimization_barrier((array, *others))[0] if others else array


def gathered_place(distance, order):
    place = jnp.zeros_like(distance)
    for step, mask in enumerate(order):
        place = place + jnp.where((distance & mask) != 0, 1 << step, 0)
    return place


def transpose_kernel(src, dst):
    for t in range(src.shape[0]):
        dst[t] = src[t].T


def tile_of(values):
    return jnp.pad(values.astype(jnp.bfloat16)[None, :], ((0, pad - 1), (0, 128 - values.shape[0])))


def row_slice(ref, start, size):
    return ref[pl.ds(pl.multiple_of(start, pad), size), :]


def side(blocks):
    return jnp.concatenate(blocks, axis=1)


def assemble(pieces, sems):
    copies = [
        pltpu.make_async_copy(
            source.at[pl.ds(at, size), :], target.at[pl.ds(to, size), :], sems.at[n]
        )
        for n, (source, at, size, target, to) in enumerate(pieces)
    ]
    for copy in copies:
        copy.start()
    return copies


def left_kernel(layout, rows, per_quarter, block, half, index, prior, *refs):
    first, second, p1, p2, weights, first_next, sems = refs[-7:]
    targets = (p1, p2, weights)
    count = half * per_quarter
    copies = assemble(
        [(refs[n], at, size, targets[which], to) for n, at, size, which, to in layout], sems
    )
    at_next = rows
    at_pick = at_next + half
    at_pick_next = at_pick + rows * per_quarter

    def row_weights(offset):
        return side([row_slice(weights, offset, block), row_slice(weights, offset + block, block)])

    def blk(ref, n):
        return ref[pl.ds(pl.multiple_of(n * block, block), block), :]

    zero = jnp.zeros((block, block), jnp.bfloat16)
    for ref in (p1, p2, first_next):
        ref[pl.ds(count * block, block), :] = zero
    for copy, (_, _, _, which, _) in zip(copies, layout):
        if which != 1:
            copy.wait()
    for i in range(rows):
        own = side([prior[i, k] for k in range(per_quarter)])
        cross = side([blk(p1, index[at_pick + i * per_quarter + k]) for k in range(per_quarter)])
        first[i] = jnp.dot(
            row_weights(index[i]),
            jnp.concatenate([own, cross], axis=0),
            preferred_element_type=jnp.float32,
        ).astype(jnp.bfloat16)
    for copy, (_, _, _, which, _) in zip(copies, layout):
        if which == 1:
            copy.wait()
    for j in range(half):
        top = side([blk(p1, j * per_quarter + k) for k in range(per_quarter)])
        low = side([blk(p2, index[at_pick_next + j * per_quarter + k]) for k in range(per_quarter)])
        got = jnp.dot(
            row_weights(index[at_next + j]),
            jnp.concatenate([top, low], axis=0),
            preferred_element_type=jnp.float32,
        ).astype(jnp.bfloat16)
        for k in range(per_quarter):
            first_next[pl.ds((j * per_quarter + k) * block, block), :] = got[:, k * block : (k + 1) * block]
    for i in range(rows):
        cross = side([blk(first_next, index[at_pick + i * per_quarter + k]) for k in range(per_quarter)])
        second[i] = jnp.dot(
            row_weights(index[i]),
            jnp.concatenate([first[i], cross], axis=0),
            preferred_element_type=jnp.float32,
        ).astype(jnp.bfloat16)


def right_kernel(layout, rows, per_quarter, block, groups, index, prior, first, second, *refs):
    out, targets, swept, result, sems, out_sems = refs[-6:]
    copies = assemble([(refs[n], at, size, targets, to) for n, at, size, to in layout], sems)
    for copy in copies:
        copy.wait()

    def target(i, k):
        return targets[pl.ds(pl.multiple_of(index[i * per_quarter + k] * block, block), block), :]

    def cut(k):
        return slice(k * block, (k + 1) * block)

    per_group = rows // groups
    sent = []
    for g in range(groups):
        mine = range(g * per_group, (g + 1) * per_group)
        for i in mine:
            for k in range(per_quarter):
                image = jnp.dot(second[i, :, cut(k)], target(i, k), preferred_element_type=jnp.float32)
                swept[i, :, cut(k)] = (
                    mixing * image + (1.0 - mixing) * first[i, :, cut(k)].astype(jnp.float32)
                ).astype(jnp.bfloat16)
        for i in mine:
            for k in range(per_quarter):
                last = jnp.dot(swept[i, :, cut(k)], target(i, k), preferred_element_type=jnp.float32)
                result[i, k] = (
                    mixing * last + (1.0 - mixing) * prior[i, k].astype(jnp.float32)
                ).astype(jnp.bfloat16)
        span = pl.ds(g * per_group, per_group)
        copy = pltpu.make_async_copy(result.at[span], out.at[span], out_sems.at[g])
        copy.start()
        sent.append(copy)
    for copy in sent:
        copy.wait()


def local(prior, candidates, cross_link, a1_blocks, a2_blocks):
    rows, per_quarter, block = prior.shape[:3]
    here = a2_blocks.shape[0]
    slabs = lax.axis_size("rows")
    quarters = lax.axis_size("cols")
    slab = lax.axis_index("rows")
    quarter = lax.axis_index("cols")
    half = rows // 2
    share = a1_blocks.shape[0]
    part = share // 2
    count = half * per_quarter
    sizes = plan["sizes"]
    chunks = len(sizes)
    starts = [sum(sizes[:c]) for c in range(chunks)]
    even = slab % 2 == 0
    there = {}

    def gated(array, name):
        return after(array, *[there[n] for n in plan["gates"].get(name, ()) if n in there])

    def record(name, array):
        there[name] = array
        return array

    target_slab = candidates >> bits_of(quarters * here)
    target_local = candidates & (here - 1)
    t_rows = here * block
    anywhere = pl.BlockSpec(memory_space=pl.ANY)
    whole = pl.BlockSpec(memory_space=pltpu.VMEM)
    scalars = pl.BlockSpec(memory_space=pltpu.SMEM)

    mine = [
        prior[half + starts[c] : half + starts[c] + sizes[c]].reshape(-1, block) for c in range(chunks)
    ]
    links = cross_link % rows - half
    own_weights = jnp.concatenate([a1_blocks.reshape(-1, block), tile_of(links)], axis=0)
    parts = [
        jnp.concatenate(
            [a1_blocks[c * part : (c + 1) * part].reshape(-1, block), tile_of(links[c * part : (c + 1) * part])],
            axis=0,
        )
        for c in range(2)
    ]
    if plan["parts_later"]:
        parts = [after(array, *mine) for array in parts]
    turned = pl.pallas_call(
        transpose_kernel, out_shape=jax.ShapeDtypeStruct(a2_blocks.shape, a2_blocks.dtype)
    )(a2_blocks).reshape(-1, block)

    far, near = {}, {}
    column = {}

    def do_far(c):
        payload = mine[c]
        got = taken_from(gated(payload, "Z%d" % c), "rows", 2)
        far[c] = record("Z%d" % c, got)

    def do_near(c):
        payload = jnp.where(even, far[c], mine[c])
        near[c] = record("Y%d" % c, exchange(gated(payload, "Y%d" % c), "rows", 1))

    def do_pair():
        got = record("T", exchange(gated(turned, "T"), "rows", 1))
        column[0] = jnp.concatenate([turned, got], axis=0)

    def do_column(d):
        column[d] = record("E%d" % d, taken_from(gated(column[0], "E%d" % d), "rows", 2 * d))

    both = ("rows", "cols")
    upper = range(quarters // 2, quarters)
    kept = [(((s + 1) % slabs) * quarters + q, s * quarters + q) for s in range(slabs) for q in upper]
    moved = [
        (((s + 1) % slabs) * quarters + q, s * quarters + q - quarters // 2)
        for s in range(slabs)
        for q in upper
    ]
    column_order = [1 << b for b in reversed(range(bits_of(quarters)))]
    w = {}

    def do_next():
        w["kept"] = record("K", lax.ppermute(gated(parts[0], "K"), both, kept))
        w["moved"] = record("M", lax.ppermute(gated(parts[1], "M"), both, moved))

    def do_columns():
        next_part = jnp.where(quarter >= quarters // 2, w["kept"], w["moved"])
        base = jnp.concatenate([own_weights, next_part], axis=0)
        w["pieces"] = [base]
        for n, mask in enumerate(column_order):
            got = record("X%d" % n, exchange(gated(base, "X%d" % n), "cols", mask))
            w["pieces"].append(got)
            base = jnp.concatenate([base, got], axis=0)
        w["all"] = base

    few = slabs == 8
    if few:
        distances = range(1, slabs // 2)
    else:
        distances = ()

    def do_ids():
        for ahead in (1, 2):
            record("I%d" % ahead, taken_from(gated(candidates[half:], "I%d" % ahead), "rows", ahead))

    for name in plan["order"]:
        if name[0] == "Z":
            do_far(int(name[1:]))
        elif name[0] == "Y":
            do_near(int(name[1:]))
        elif name == "I":
            do_ids()
        elif name == "KM":
            do_next()
        elif name == "X":
            do_columns()
        elif name[0] == "E" and few:
            do_column(int(name[1:]))
        elif name == "T" and few:
            do_pair()
    row_order = [1 << b for b in range(1, bits_of(slabs))]
    if not few:
        base = turned
        for mask in row_order:
            base = jnp.concatenate([base, exchange(base, "rows", mask)], axis=0)
        swapped = exchange(base, "rows", 1)

    own_rows = own_weights.shape[0]
    share_rows = own_rows + parts[0].shape[0]
    tiles = w["all"].reshape(quarters, share_rows, block)
    row_quarter = jnp.arange(quarters, dtype=jnp.int32)
    place = gathered_place(row_quarter ^ quarter, column_order)

    def taken(table, at):
        same = at[..., None] == jnp.arange(table.shape[0], dtype=jnp.int32)
        return jnp.sum(
            jnp.where(same.reshape(same.shape + (1,) * (table.ndim - 1)), table, 0), axis=at.ndim
        )

    link_own = taken(tiles[:, own_rows - pad, :share].astype(jnp.int32), place).reshape(-1)
    offset_own = (
        place[:, None] * share_rows + jnp.arange(share, dtype=jnp.int32)[None, :] * 2 * block
    ).reshape(-1)
    next_index = jnp.arange(half, dtype=jnp.int32)
    source = quarters // 2 + next_index // share
    inside = next_index % share
    holder = jnp.where(inside < part, source, source - quarters // 2)
    holder_place = gathered_place(holder ^ quarter, column_order)
    inside = inside % part
    link_next = taken(
        tiles[:, share_rows - pad, :part].astype(jnp.int32).reshape(-1), holder_place * part + inside
    )
    offset_next = holder_place * share_rows + own_rows + inside * 2 * block

    def picked(ours, theirs, link):
        same = ours[:, :, None] == taken(theirs, link)[:, None, :]
        which = jnp.sum(
            jnp.where(same, jnp.arange(per_quarter, dtype=jnp.int32)[None, None, :], 0), axis=2
        )
        return jnp.where(jnp.any(same, axis=2), link[:, None] * per_quarter + which, count)

    pick_own = picked(candidates, there["I1"], link_own)
    pick_next = picked(there["I1"], there["I2"], link_next)
    index = jnp.concatenate(
        [offset_own, offset_next, pick_own.reshape(-1), pick_next.reshape(-1)]
    )
    odd_one = (target_slab ^ slab) & 1
    base_slab = slab ^ odd_one
    if few:
        ahead = ((target_slab - base_slab) % slabs) // 2
    else:
        ahead = gathered_place(target_slab ^ base_slab, row_order)
    target_place = (odd_one * (slabs // 2) + ahead) * here + target_local
    t_index = target_place.reshape(-1)

    params = pltpu.CompilerParams(vmem_limit_bytes=plan["vmem"] * 1024 * 1024)

    plan_space = anywhere if plan["any"] else whole
    arrays, layout = [], []

    def piece(array, at, size, *where):
        for n, known in enumerate(arrays):
            if known is array:
                break
        else:
            n = len(arrays)
            arrays.append(array)
        layout.append((n, at, size, *where))

    for c in range(chunks):
        size = sizes[c] * per_quarter * block
        piece(near[c], 0, size, 0, starts[c] * per_quarter * block)
    to = 0
    for array in w["pieces"]:
        piece(array, 0, array.shape[0], 2, to)
        to += array.shape[0]
    for c in range(chunks):
        size = sizes[c] * per_quarter * block
        piece(far[c], 0, size, 1, starts[c] * per_quarter * block)
    wide = jax.ShapeDtypeStruct((rows, block, per_quarter * block), jnp.bfloat16)
    stack = pltpu.VMEM(((count + 1) * block, block), jnp.bfloat16)
    first, second = pl.pallas_call(
        functools.partial(left_kernel, tuple(layout), rows, per_quarter, block, half),
        in_specs=[scalars, whole] + [plan_space] * len(arrays),
        out_specs=[whole, whole],
        out_shape=[wide, wide],
        scratch_shapes=[
            stack,
            stack,
            pltpu.VMEM((to, block), jnp.bfloat16),
            stack,
            pltpu.SemaphoreType.DMA((len(layout),)),
        ],
        compiler_params=params,
        cost_estimate=pl.CostEstimate(flops=plan["cost"] * 10**9, bytes_accessed=8 * 2**20, transcendentals=0),
    )(index, prior, *arrays)

    arrays, layout = [], []
    if few:
        for d in range(slabs // 2):
            piece(column[d], 0, t_rows, d * t_rows)
            piece(column[d], t_rows, t_rows, (slabs // 2 + d) * t_rows)
    else:
        piece(base, 0, base.shape[0], 0)
        piece(swapped, 0, base.shape[0], base.shape[0])
    groups = plan["groups"]
    return pl.pallas_call(
        functools.partial(right_kernel, tuple(layout), rows, per_quarter, block, groups),
        in_specs=[scalars, whole, whole, whole] + [plan_space] * len(arrays),
        out_specs=anywhere,
        out_shape=jax.ShapeDtypeStruct(prior.shape, prior.dtype),
        scratch_shapes=[
            pltpu.VMEM((slabs * t_rows, block), jnp.bfloat16),
            pltpu.VMEM(wide.shape, jnp.bfloat16),
            pltpu.VMEM(prior.shape, jnp.bfloat16),
            pltpu.SemaphoreType.DMA((len(layout),)),
            pltpu.SemaphoreType.DMA((groups,)),
        ],
        compiler_params=params,
        cost_estimate=pl.CostEstimate(flops=10**9, bytes_accessed=8 * 2**20, transcendentals=0),
    )(t_index, prior, first, second, *arrays)


def solution(mesh):
    placed = (
        P("rows", "cols", None, None),
        P("rows", "cols"),
        P(("rows", "cols")),
        P(("rows", "cols"), None, None, None),
        P(("rows", "cols"), None, None),
    )
    return jax.shard_map(
        local, mesh=mesh, in_specs=placed, out_specs=P("rows", "cols", None, None), check_vma=False
    )
```

```python
import functools

import jax
import jax.numpy as jnp
from jax import lax
from jax.experimental import pallas as pl
from jax.experimental.pallas import tpu as pltpu
from jax.sharding import PartitionSpec as P

mixing = 0.75
pad = 16
plan = {'sizes': (4, 4),
 'gates': {'Y1': ['Y0'], 'T': ['Z0'], 'I1': ['T'], 'I2': ['T'], 'E1': ['Y0'], 'E3': ['Y0']},
 'order': ['Z0', 'Z1', 'KM', 'T', 'I', 'X', 'Y0', 'Y1', 'E1', 'E2', 'E3'],
 'cost': 0,
 'groups': 2,
 'vmem': 48,
 'any': True,
 'parts_later': False}


def bits_of(count):
    return count.bit_length() - 1


def exchange(array, axis, mask):
    count = lax.axis_size(axis)
    return lax.ppermute(array, axis, [(i, i ^ mask) for i in range(count)])


def taken_from(array, axis, ahead):
    count = lax.axis_size(axis)
    return lax.ppermute(array, axis, [(i, (i - ahead) % count) for i in range(count)])


def after(array, *others):
    return lax.optimization_barrier((array, *others))[0] if others else array


def gathered_place(distance, order):
    place = jnp.zeros_like(distance)
    for step, mask in enumerate(order):
        place = place + jnp.where((distance & mask) != 0, 1 << step, 0)
    return place


def transpose_kernel(src, dst):
    for t in range(src.shape[0]):
        dst[t] = src[t].T


def tile_of(values):
    return jnp.pad(values.astype(jnp.bfloat16)[None, :], ((0, pad - 1), (0, 128 - values.shape[0])))


def row_slice(ref, start, size):
    return ref[pl.ds(pl.multiple_of(start, pad), size), :]


def side(blocks):
    return jnp.concatenate(blocks, axis=1)


def assemble(pieces, sems):
    copies = [
        pltpu.make_async_copy(
            source.at[pl.ds(at, size), :], target.at[pl.ds(to, size), :], sems.at[n]
        )
        for n, (source, at, size, target, to) in enumerate(pieces)
    ]
    for copy in copies:
        copy.start()
    return copies


def left_kernel(layout, rows, per_quarter, block, half, index, prior, *refs):
    first, second, p1, p2, weights, first_next, sems = refs[-7:]
    targets = (p1, p2, weights)
    count = half * per_quarter
    copies = assemble(
        [(refs[n], at, size, targets[which], to) for n, at, size, which, to in layout], sems
    )
    at_next = rows
    at_pick = at_next + half
    at_pick_next = at_pick + rows * per_quarter

    def row_weights(offset):
        return side([row_slice(weights, offset, block), row_slice(weights, offset + block, block)])

    def blk(ref, n):
        return ref[pl.ds(pl.multiple_of(n * block, block), block), :]

    zero = jnp.zeros((block, block), jnp.bfloat16)
    for ref in (p1, p2, first_next):
        ref[pl.ds(count * block, block), :] = zero
    for copy, (_, _, _, which, _) in zip(copies, layout):
        if which != 1:
            copy.wait()
    for i in range(rows):
        own = side([prior[i, k] for k in range(per_quarter)])
        cross = side([blk(p1, index[at_pick + i * per_quarter + k]) for k in range(per_quarter)])
        first[i] = jnp.dot(
            row_weights(index[i]),
            jnp.concatenate([own, cross], axis=0),
            preferred_element_type=jnp.float32,
        ).astype(jnp.bfloat16)
    for copy, (_, _, _, which, _) in zip(copies, layout):
        if which == 1:
            copy.wait()
    for j in range(half):
        top = side([blk(p1, j * per_quarter + k) for k in range(per_quarter)])
        low = side([blk(p2, index[at_pick_next + j * per_quarter + k]) for k in range(per_quarter)])
        got = jnp.dot(
            row_weights(index[at_next + j]),
            jnp.concatenate([top, low], axis=0),
            preferred_element_type=jnp.float32,
        ).astype(jnp.bfloat16)
        for k in range(per_quarter):
            first_next[pl.ds((j * per_quarter + k) * block, block), :] = got[:, k * block : (k + 1) * block]
    for i in range(rows):
        cross = side([blk(first_next, index[at_pick + i * per_quarter + k]) for k in range(per_quarter)])
        second[i] = jnp.dot(
            row_weights(index[i]),
            jnp.concatenate([first[i], cross], axis=0),
            preferred_element_type=jnp.float32,
        ).astype(jnp.bfloat16)


def right_kernel(layout, rows, per_quarter, block, groups, index, prior, first, second, *refs):
    out, targets, swept, result, sems, out_sems = refs[-6:]
    copies = assemble([(refs[n], at, size, targets, to) for n, at, size, to in layout], sems)
    for copy in copies:
        copy.wait()

    def target(i, k):
        return targets[pl.ds(pl.multiple_of(index[i * per_quarter + k] * block, block), block), :]

    def cut(k):
        return slice(k * block, (k + 1) * block)

    per_group = rows // groups
    sent = []
    for g in range(groups):
        mine = range(g * per_group, (g + 1) * per_group)
        for i in mine:
            for k in range(per_quarter):
                image = jnp.dot(second[i, :, cut(k)], target(i, k), preferred_element_type=jnp.float32)
                swept[i, :, cut(k)] = (
                    mixing * image + (1.0 - mixing) * first[i, :, cut(k)].astype(jnp.float32)
                ).astype(jnp.bfloat16)
        for i in mine:
            for k in range(per_quarter):
                last = jnp.dot(swept[i, :, cut(k)], target(i, k), preferred_element_type=jnp.float32)
                result[i, k] = (
                    mixing * last + (1.0 - mixing) * prior[i, k].astype(jnp.float32)
                ).astype(jnp.bfloat16)
        span = pl.ds(g * per_group, per_group)
        copy = pltpu.make_async_copy(result.at[span], out.at[span], out_sems.at[g])
        copy.start()
        sent.append(copy)
    for copy in sent:
        copy.wait()


def local(prior, candidates, cross_link, a1_blocks, a2_blocks):
    rows, per_quarter, block = prior.shape[:3]
    here = a2_blocks.shape[0]
    slabs = lax.axis_size("rows")
    quarters = lax.axis_size("cols")
    slab = lax.axis_index("rows")
    quarter = lax.axis_index("cols")
    half = rows // 2
    share = a1_blocks.shape[0]
    part = share // 2
    count = half * per_quarter
    sizes = plan["sizes"]
    chunks = len(sizes)
    starts = [sum(sizes[:c]) for c in range(chunks)]
    even = slab % 2 == 0
    there = {}

    def gated(array, name):
        return after(array, *[there[n] for n in plan["gates"].get(name, ()) if n in there])

    def record(name, array):
        there[name] = array
        return array

    target_slab = candidates >> bits_of(quarters * here)
    target_local = candidates & (here - 1)
    t_rows = here * block
    anywhere = pl.BlockSpec(memory_space=pl.ANY)
    whole = pl.BlockSpec(memory_space=pltpu.VMEM)
    scalars = pl.BlockSpec(memory_space=pltpu.SMEM)

    mine = [
        prior[half + starts[c] : half + starts[c] + sizes[c]].reshape(-1, block) for c in range(chunks)
    ]
    links = cross_link % rows - half
    own_weights = jnp.concatenate([a1_blocks.reshape(-1, block), tile_of(links)], axis=0)
    parts = [
        jnp.concatenate(
            [a1_blocks[c * part : (c + 1) * part].reshape(-1, block), tile_of(links[c * part : (c + 1) * part])],
            axis=0,
        )
        for c in range(2)
    ]
    if plan["parts_later"]:
        parts = [after(array, *mine) for array in parts]
    turned = pl.pallas_call(
        transpose_kernel, out_shape=jax.ShapeDtypeStruct(a2_blocks.shape, a2_blocks.dtype)
    )(a2_blocks).reshape(-1, block)

    far, near = {}, {}
    column = {}

    def do_far(c):
        payload = mine[c]
        got = taken_from(gated(payload, "Z%d" % c), "rows", 2)
        far[c] = record("Z%d" % c, got)

    def do_near(c):
        payload = jnp.where(even, far[c], mine[c])
        near[c] = record("Y%d" % c, exchange(gated(payload, "Y%d" % c), "rows", 1))

    def do_pair():
        got = record("T", exchange(gated(turned, "T"), "rows", 1))
        column[0] = jnp.concatenate([turned, got], axis=0)

    def do_column(d):
        column[d] = record("E%d" % d, taken_from(gated(column[0], "E%d" % d), "rows", 2 * d))

    both = ("rows", "cols")
    upper = range(quarters // 2, quarters)
    kept = [(((s + 1) % slabs) * quarters + q, s * quarters + q) for s in range(slabs) for q in upper]
    moved = [
        (((s + 1) % slabs) * quarters + q, s * quarters + q - quarters // 2)
        for s in range(slabs)
        for q in upper
    ]
    column_order = [1 << b for b in reversed(range(bits_of(quarters)))]
    w = {}

    def do_next():
        w["kept"] = record("K", lax.ppermute(gated(parts[0], "K"), both, kept))
        w["moved"] = record("M", lax.ppermute(gated(parts[1], "M"), both, moved))

    def do_columns():
        next_part = jnp.where(quarter >= quarters // 2, w["kept"], w["moved"])
        base = jnp.concatenate([own_weights, next_part], axis=0)
        w["pieces"] = [base]
        for n, mask in enumerate(column_order):
            got = record("X%d" % n, exchange(gated(base, "X%d" % n), "cols", mask))
            w["pieces"].append(got)
            base = jnp.concatenate([base, got], axis=0)
        w["all"] = base

    few = slabs == 8
    if few:
        distances = range(1, slabs // 2)
    else:
        distances = ()

    def do_ids():
        for ahead in (1, 2):
            record("I%d" % ahead, taken_from(gated(candidates[half:], "I%d" % ahead), "rows", ahead))

    for name in plan["order"]:
        if name[0] == "Z":
            do_far(int(name[1:]))
        elif name[0] == "Y":
            do_near(int(name[1:]))
        elif name == "I":
            do_ids()
        elif name == "KM":
            do_next()
        elif name == "X":
            do_columns()
        elif name[0] == "E" and few:
            do_column(int(name[1:]))
        elif name == "T" and few:
            do_pair()
    row_order = [1 << b for b in range(1, bits_of(slabs))]
    if not few:
        base = turned
        for mask in row_order:
            base = jnp.concatenate([base, exchange(base, "rows", mask)], axis=0)
        swapped = exchange(base, "rows", 1)

    own_rows = own_weights.shape[0]
    share_rows = own_rows + parts[0].shape[0]
    tiles = w["all"].reshape(quarters, share_rows, block)
    row_quarter = jnp.arange(quarters, dtype=jnp.int32)
    place = gathered_place(row_quarter ^ quarter, column_order)

    def taken(table, at):
        same = at[..., None] == jnp.arange(table.shape[0], dtype=jnp.int32)
        return jnp.sum(
            jnp.where(same.reshape(same.shape + (1,) * (table.ndim - 1)), table, 0), axis=at.ndim
        )

    link_own = taken(tiles[:, own_rows - pad, :share].astype(jnp.int32), place).reshape(-1)
    offset_own = (
        place[:, None] * share_rows + jnp.arange(share, dtype=jnp.int32)[None, :] * 2 * block
    ).reshape(-1)
    next_index = jnp.arange(half, dtype=jnp.int32)
    source = quarters // 2 + next_index // share
    inside = next_index % share
    holder = jnp.where(inside < part, source, source - quarters // 2)
    holder_place = gathered_place(holder ^ quarter, column_order)
    inside = inside % part
    link_next = taken(
        tiles[:, share_rows - pad, :part].astype(jnp.int32).reshape(-1), holder_place * part + inside
    )
    offset_next = holder_place * share_rows + own_rows + inside * 2 * block

    def picked(ours, theirs, link):
        same = ours[:, :, None] == taken(theirs, link)[:, None, :]
        which = jnp.sum(
            jnp.where(same, jnp.arange(per_quarter, dtype=jnp.int32)[None, None, :], 0), axis=2
        )
        return jnp.where(jnp.any(same, axis=2), link[:, None] * per_quarter + which, count)

    pick_own = picked(candidates, there["I1"], link_own)
    pick_next = picked(there["I1"], there["I2"], link_next)
    index = jnp.concatenate(
        [offset_own, offset_next, pick_own.reshape(-1), pick_next.reshape(-1)]
    )
    odd_one = (target_slab ^ slab) & 1
    base_slab = slab ^ odd_one
    if few:
        ahead = ((target_slab - base_slab) % slabs) // 2
    else:
        ahead = gathered_place(target_slab ^ base_slab, row_order)
    target_place = (odd_one * (slabs // 2) + ahead) * here + target_local
    t_index = target_place.reshape(-1)

    params = pltpu.CompilerParams(vmem_limit_bytes=plan["vmem"] * 1024 * 1024)

    plan_space = anywhere if plan["any"] else whole
    arrays, layout = [], []

    def piece(array, at, size, *where):
        for n, known in enumerate(arrays):
            if known is array:
                break
        else:
            n = len(arrays)
            arrays.append(array)
        layout.append((n, at, size, *where))

    for c in range(chunks):
        size = sizes[c] * per_quarter * block
        piece(near[c], 0, size, 0, starts[c] * per_quarter * block)
    to = 0
    for array in w["pieces"]:
        piece(array, 0, array.shape[0], 2, to)
        to += array.shape[0]
    for c in range(chunks):
        size = sizes[c] * per_quarter * block
        piece(far[c], 0, size, 1, starts[c] * per_quarter * block)
    wide = jax.ShapeDtypeStruct((rows, block, per_quarter * block), jnp.bfloat16)
    stack = pltpu.VMEM(((count + 1) * block, block), jnp.bfloat16)
    first, second = pl.pallas_call(
        functools.partial(left_kernel, tuple(layout), rows, per_quarter, block, half),
        in_specs=[scalars, whole] + [plan_space] * len(arrays),
        out_specs=[whole, whole],
        out_shape=[wide, wide],
        scratch_shapes=[
            stack,
            stack,
            pltpu.VMEM((to, block), jnp.bfloat16),
            stack,
            pltpu.SemaphoreType.DMA((len(layout),)),
        ],
        compiler_params=params,
        cost_estimate=pl.CostEstimate(flops=plan["cost"] * 10**9, bytes_accessed=8 * 2**20, transcendentals=0),
    )(index, prior, *arrays)

    arrays, layout = [], []
    if few:
        for d in range(slabs // 2):
            piece(column[d], 0, t_rows, d * t_rows)
            piece(column[d], t_rows, t_rows, (slabs // 2 + d) * t_rows)
    else:
        piece(base, 0, base.shape[0], 0)
        piece(swapped, 0, base.shape[0], base.shape[0])
    groups = plan["groups"]
    return pl.pallas_call(
        functools.partial(right_kernel, tuple(layout), rows, per_quarter, block, groups),
        in_specs=[scalars, whole, whole, whole] + [plan_space] * len(arrays),
        out_specs=anywhere,
        out_shape=jax.ShapeDtypeStruct(prior.shape, prior.dtype),
        scratch_shapes=[
            pltpu.VMEM((slabs * t_rows, block), jnp.bfloat16),
            pltpu.VMEM(wide.shape, jnp.bfloat16),
            pltpu.VMEM(prior.shape, jnp.bfloat16),
            pltpu.SemaphoreType.DMA((len(layout),)),
            pltpu.SemaphoreType.DMA((groups,)),
        ],
        compiler_params=params,
        cost_estimate=pl.CostEstimate(flops=10**9, bytes_accessed=8 * 2**20, transcendentals=0),
    )(t_index, prior, first, second, *arrays)


def solution(mesh):
    placed = (
        P("rows", "cols", None, None),
        P("rows", "cols"),
        P(("rows", "cols")),
        P(("rows", "cols"), None, None, None),
        P(("rows", "cols"), None, None),
    )
    return jax.shard_map(
        local, mesh=mesh, in_specs=placed, out_specs=P("rows", "cols", None, None), check_vma=False
    )
```
